32 devices in a mesh: dp: 4 (over y, x), expert: 8 (over z, core).
Axes of the slice: x: 2, y: 2, z: 4, core: 2. Of those that a mesh axis runs over, the one named last changes fastest.
Arguments:
- tokens: bfloat16 [1024, 6144], P('expert', 'dp'), may hold values from -6 to 6
- expert_ids: int32 [1024, 4], P('expert'), may hold values from 0 to 7, all different within a row; in each aligned block of 128 rows (0 to 127, 128 to 255, ...) at most 96 rows name the same one
- route_weights: float32 [1024, 4], P('expert'), may hold values from 0.2 to 1
- gate_weights: bfloat16 [8, 6144, 2048], P('expert', None, 'dp'), may hold values from -0.078125 to 0.078125
- up_weights: bfloat16 [8, 6144, 2048], P('expert', None, 'dp'), may hold values from -0.078125 to 0.078125
- down_weights: bfloat16 [8, 2048, 6144], P('expert', 'dp'), may hold values from -0.125 to 0.125
- grad_out: bfloat16 [1024, 6144], P('expert', 'dp'), may hold values from -6 to 6
Outputs:
- mixed: bfloat16 [1024, 6144], P('expert', 'dp')
- token_grad: bfloat16 [1024, 6144], P('expert', 'dp')
- route_grad: float32 [1024, 4], P('expert')
- gate_grad: bfloat16 [8, 6144, 2048], P('expert', None, 'dp')
- up_grad: bfloat16 [8, 6144, 2048], P('expert', None, 'dp')
- down_grad: bfloat16 [8, 2048, 6144], P('expert', 'dp')
The draws below stay inside these ranges and needn't reach their ends.
Inputs may be any that keep to these rules, and one draw needn't show every extreme that they name: `expert_ids`: the 4 experts of a token differ; in every block of 128 consecutive tokens (the tokens of one index of the expert axis) no expert is chosen by more than 96 tokens, and some expert is chosen by exactly 96 in some blocks.
All inputs are finite; a program needn't handle non-finite values.
Results may differ from the reference program's by a relative error of at most 0.014.
Values may be sent and summed in bfloat16 or wider, within the bound.
A program may use at most 192 MiB of HBM per device.

```python
import math
import jax
import jax.numpy as jnp
import numpy as np
from jax import lax

D = 6144
FF = 2048
TOP = 4
TOK_DEV = 128
EXPERTS = 8
SLOT = 96
TOKENS = 1024
N_DP = 4
N_EXPERT = 8


def block_levels(own_key, extent, pieces, least, top_value):
    loudness, own = 1.0, jax.random.fold_in(own_key, 6)
    for position, blocks in pieces:
        heights = jnp.exp(jax.random.uniform(jax.random.fold_in(own, position), (blocks,), jnp.float32, least / len(pieces), top_value / len(pieces)))
        loudness = loudness * jnp.repeat(heights, extent[position] // blocks).reshape([-1 if axis == position else 1 for axis in range(len(extent))])
    return loudness


def routed_block(rng, own, number, rows, count, top, bound, slope):
    order = jax.random.permutation(rng, count)
    crowded, ordinary = load_shares(count, rows * top, bound, slope, True), load_shares(count, rows * top, bound, slope, False)
    places = jnp.arange(count)

    def named(lengths, offset_by):
        used = int((lengths > 0).sum())
        fixed = max(1, used // 4)
        moved = fixed + (places - fixed + offset_by * (used - fixed)) % max(1, count - fixed)
        return jnp.zeros((count,), jnp.int32).at[order[jnp.where(places < fixed, places, moved)]].set(jnp.asarray(lengths, jnp.int32))

    lengths = jnp.where(number % 4 == 0, named(crowded, number // 4), named(ordinary, number - number // 4 - 1))
    mixed = jax.random.permutation(jax.random.fold_in(own, 3), count)
    giver, receiver = mixed[0:count // 2 * 2:2], mixed[1:count // 2 * 2:2]
    slack = jnp.minimum(lengths[giver] - 1, bound - lengths[receiver]) // 2
    slack = jnp.where((giver == order[0]) | (receiver == order[0]) | (lengths[receiver] == 0), 0, jnp.maximum(slack, 0))
    moved = jax.random.randint(jax.random.fold_in(own, 4), (count // 2,), 0, 1 << 20) % (slack + 1)
    lengths = lengths.at[giver].add(-moved).at[receiver].add(moved)
    items = jnp.searchsorted(jnp.cumsum(lengths), jnp.arange(rows * top), side="right").astype(jnp.int32)
    listing = items.reshape(top, rows).T
    listing = listing[jax.random.permutation(jax.random.fold_in(own, 1), rows)]
    offset_by = jax.random.randint(jax.random.fold_in(own, 2), (rows, 1), 0, top)
    return jnp.take_along_axis(listing, (jnp.arange(top)[None, :] + offset_by) % top, axis=1)


def load_shares(count, total, most, slope, full):
    loads = [(1 << 20) // math.isqrt(grade ** slope) + 1 for grade in range(1, count + 1)]
    largest = most if full else min(most, max(-(-total // count), total * loads[0] // sum(loads)))
    least = 1 if total - largest >= count - 1 else 0
    holding, spare = [largest] + [least] * (count - 1), total - largest - least * (count - 1)
    while spare > 0:
        free = [i for i in range(1, count) if holding[i] < largest] or [i for i in range(1, count) if holding[i] < most]
        mass, left = sum([loads[i] for i in free]), spare
        for i in free:
            more = min(most - holding[i], max(1, left * loads[i] // mass), spare)
            holding[i] = holding[i] + more
            spare = spare - more
    return np.array(holding)


def normal_values(rng, shape, spread, reach, split=(), held_as=jnp.bfloat16):
    result = jax.random.normal(rng, shape, jnp.float32) * spread
    if len(split) > 0:
        result = block_levels(rng, shape, split, -0.22, 0.18) * result
    return jnp.clip(result, min=-reach, max=reach).astype(held_as)


def setup_inputs(seed: int = 0) -> dict:
    keys = jax.random.split(jax.random.key(seed), 8)
    tokens = normal_values(keys[0], (TOKENS, D), 1.0, 6.0, ((0, 8), (1, 4)))
    expert_ids_keys = jax.random.split(jax.random.fold_in(keys[1], 1), TOKENS // TOK_DEV)
    expert_ids_turns = jax.random.permutation(jax.random.fold_in(keys[1], 3), TOKENS // TOK_DEV)
    expert_ids = jax.vmap(lambda own, number: routed_block(jax.random.fold_in(keys[1], 2), own, number, TOK_DEV, EXPERTS, TOP, SLOT, 2))(expert_ids_keys, expert_ids_turns).reshape((TOKENS, TOP))
    route_weights = jnp.clip(0.2 + 0.8 * jax.random.uniform(keys[2], (TOKENS, TOP), jnp.float32) ** block_levels(keys[2], (TOKENS, TOP), ((0, 8),), -0.2, 0.2), 0.2, 1.0)
    gate_weights = normal_values(keys[3], (EXPERTS, D, FF), D ** -0.5, 0.078125, ((0, 8), (2, 4)))
    up_weights = normal_values(keys[4], (EXPERTS, D, FF), D ** -0.5, 0.078125, ((0, 8), (2, 4)))
    down_weights = normal_values(keys[5], (EXPERTS, FF, D), FF ** -0.5, 0.125, ((0, 8), (1, 4)))
    grad_out = normal_values(keys[6], (TOKENS, D), 1.0, 6.0, ((0, 8), (1, 4)))
    return dict(tokens=tokens, expert_ids=expert_ids, route_weights=route_weights, gate_weights=gate_weights, up_weights=up_weights, down_weights=down_weights, grad_out=grad_out)


def reference(tokens, expert_ids, route_weights, gate_weights, up_weights, down_weights, grad_out):
    assigned = TOKENS * TOP
    capacity = min(TOKENS, N_EXPERT * SLOT)
    group_width = FF // N_DP
    flat_ids = expert_ids.reshape(assigned)
    scaled = (route_weights[:, :, None] * grad_out[:, None, :].astype(jnp.float32)).astype(jnp.bfloat16).reshape(assigned, D)
    contract_last = (((1,), (1,)), ((), ()))
    contract_first = (((0,), (0,)), ((), ()))

    def expert_step(totals, expert):
        outputs, input_grads = totals
        picked = jnp.nonzero(flat_ids == expert, size=capacity, fill_value=assigned)[0].astype(jnp.int32)
        usable = picked < assigned
        safe_index = jnp.where(usable, picked, 0).astype(jnp.int32)
        inputs = jnp.where(usable[:, None], tokens[safe_index // TOP], jnp.zeros((), jnp.bfloat16))
        gate_weight = gate_weights[expert]
        up_weight = up_weights[expert]
        down_weight = down_weights[expert]
        gate_pre = jnp.dot(inputs, gate_weight, preferred_element_type=jnp.float32)
        up_pre = jnp.dot(inputs, up_weight, preferred_element_type=jnp.float32)
        gate_sigmoid = jax.nn.sigmoid(gate_pre)
        hidden = (gate_pre * gate_sigmoid * up_pre).astype(jnp.bfloat16)
        out_total = jnp.zeros((capacity, D), jnp.float32)
        for group in range(N_DP):
            low = group * group_width
            part = jnp.dot(hidden[:, low:low + group_width], down_weight[low:low + group_width],
                           preferred_element_type=jnp.float32).astype(jnp.bfloat16)
            out_total = out_total + lax.optimization_barrier(part).astype(jnp.float32)
        expert_out = out_total.astype(jnp.bfloat16)
        out_grad = jnp.where(usable[:, None], scaled[safe_index], jnp.zeros((), jnp.bfloat16))
        hidden_grad = lax.dot_general(out_grad, down_weight, contract_last, preferred_element_type=jnp.float32)
        grad_gate_pre = (hidden_grad * up_pre * gate_sigmoid * (1.0 + gate_pre * (1.0 - gate_sigmoid))).astype(jnp.bfloat16)
        grad_up_pre = (hidden_grad * gate_pre * gate_sigmoid).astype(jnp.bfloat16)
        down_grad = lax.dot_general(hidden, out_grad, contract_first, preferred_element_type=jnp.float32).astype(jnp.bfloat16)
        gate_grad = lax.dot_general(inputs, grad_gate_pre, contract_first, preferred_element_type=jnp.float32).astype(jnp.bfloat16)
        up_grad = lax.dot_general(inputs, grad_up_pre, contract_first, preferred_element_type=jnp.float32).astype(jnp.bfloat16)
        row_total = jnp.zeros((capacity, D), jnp.float32)
        for group in range(N_DP):
            low = group * group_width
            part = (lax.dot_general(grad_gate_pre[:, low:low + group_width], gate_weight[:, low:low + group_width],
                                    contract_last, preferred_element_type=jnp.float32)
                    + lax.dot_general(grad_up_pre[:, low:low + group_width], up_weight[:, low:low + group_width],
                                      contract_last, preferred_element_type=jnp.float32)).astype(jnp.bfloat16)
            row_total = row_total + lax.optimization_barrier(part).astype(jnp.float32)
        row_grad = row_total.astype(jnp.bfloat16)
        outputs = outputs.at[picked].set(expert_out, mode="drop")
        input_grads = input_grads.at[picked].set(row_grad, mode="drop")
        return (outputs, input_grads), (gate_grad, up_grad, down_grad)

    initial = (jnp.zeros((assigned, D), jnp.bfloat16), jnp.zeros((assigned, D), jnp.bfloat16))
    (outputs, input_grads), (gate_grad, up_grad, down_grad) = lax.scan(
        expert_step, initial, jnp.arange(EXPERTS, dtype=jnp.int32))
    slot_out = outputs.reshape(TOKENS, TOP, D).astype(jnp.float32)
    mixed = jnp.sum(route_weights[:, :, None] * slot_out, axis=1).astype(jnp.bfloat16)
    route_grad = jnp.sum(slot_out * grad_out[:, None, :].astype(jnp.float32), axis=2)
    token_grad = jnp.sum(input_grads.reshape(TOKENS, TOP, D).astype(jnp.float32), axis=1).astype(jnp.bfloat16)
    return (mixed, token_grad, route_grad, gate_grad, up_grad, down_grad)
```

```python
import functools
import jax
import jax.numpy as jnp
from jax import lax
from jax.experimental import pallas as pl
from jax.experimental.pallas import tpu as pltpu
from jax.sharding import PartitionSpec as P

CORES = 2
contract_last = (((1,), (1,)), ((), ()))
contract_first = (((0,), (0,)), ((), ()))


def dot32(left, right, dims=(((1,), (0,)), ((), ()))):
    return lax.dot_general(left, right, dims, preferred_element_type=jnp.float32)


def line_groups(count):
    return [[i for i in range(count) if i % CORES == core] for core in range(CORES)]


def pair_groups(count):
    return [[i + core for core in range(CORES)] for i in range(0, count, CORES)]


def gather_rows(block):
    count = lax.axis_size("expert")
    line = lax.all_gather(block, "expert", axis=0, tiled=True, axis_index_groups=line_groups(count))
    wide = lax.all_gather(line, "dp", axis=1, tiled=True)
    return lax.all_gather(wide, "expert", axis=0, tiled=True, axis_index_groups=pair_groups(count))


def scatter_rows(partial_value):
    count = lax.axis_size("expert")
    half = lax.psum_scatter(
        partial_value, "expert", scatter_dimension=0, tiled=True, axis_index_groups=pair_groups(count)
    )
    narrow = lax.psum_scatter(half, "dp", scatter_dimension=1, tiled=True)
    return lax.psum_scatter(
        narrow, "expert", scatter_dimension=0, tiled=True, axis_index_groups=line_groups(count)
    )


def position():
    d = lax.axis_index("dp")
    e = lax.axis_index("expert")
    return d, e // CORES, e % CORES


def greet(d, z, c, chips, across, along):
    barrier = pltpu.get_barrier_semaphore()

    def signal(dd, zz, cc):
        pl.semaphore_signal(
            barrier, inc=1, device_id=(dd, zz * CORES + cc), device_id_type=pl.DeviceIdType.MESH
        )

    signal(across, z, c)
    signal(along, z, c)
    signal(d, z, 1 - c)
    pl.when(z > 0)(lambda: signal(d, z - 1, c))
    pl.when(z < chips - 1)(lambda: signal(d, z + 1, c))
    inner = jnp.where(z > 0, 1, 0) + jnp.where(z < chips - 1, 1, 0)
    pl.semaphore_wait(barrier, 3 + inner)


def gather_kernel(
    chips, t_in, g_in, w_in, t_out, g_out, w_out,
    own_sem, up_s, down_s, line_r, x_s, x_r, y_s, y_r, a_s, a_r, b_s, b_r, c_s, c_r,
):
    d, z, c = position()
    across = d + 1 - 2 * (d % 2)
    along = (d + 2) % 4
    diagonal = 3 - d
    columns = (d, across, along, diagonal)
    ins = (t_in, g_in, w_in)
    outs = (t_out, g_out, w_out)
    rows, width = t_in.shape

    def place(a, cc, zz, dd, half=None):
        slot = cc * chips + zz
        if a == 2:
            return outs[a].at[slot]
        first, size = slot * rows, rows
        if half is not None:
            size = rows // 2
            first = first + half * size
        return outs[a].at[
            pl.ds(pl.multiple_of(first, rows // 2), size), pl.ds(pl.multiple_of(dd * width, width), width)
        ]

    def send(src, dst, send_sem, recv_sem, dd, zz, cc):
        return pltpu.make_async_remote_copy(
            src_ref=src, dst_ref=dst, send_sem=send_sem, recv_sem=recv_sem,
            device_id=(dd, zz * CORES + cc), device_id_type=pl.DeviceIdType.MESH,
        )

    def source(a, zz, own):
        return ins[a] if own else place(a, c, zz, d)

    def up(a, zz, own=False):
        return send(source(a, zz, own), place(a, c, zz, d), up_s.at[a, zz], line_r.at[a, zz], d, z + 1, c)

    def down(a, zz, own=False):
        return send(source(a, zz, own), place(a, c, zz, d), down_s.at[a, zz], line_r.at[a, zz], d, z - 1, c)

    def go_x(a, zz, dd, own=False):
        src = ins[a] if own else place(a, c, zz, dd)
        return send(src, place(a, c, zz, dd), x_s.at[a, zz], x_r.at[a, zz], across, z, c)

    def go_y(a, zz, dd, own=False):
        src = ins[a] if own else place(a, c, zz, dd)
        return send(src, place(a, c, zz, dd), y_s.at[a, zz], y_r.at[a, zz], along, z, c)

    def go_a(a, zz, dd):
        part = place(a, c, zz, dd, 0)
        return send(part, part, a_s.at[a, zz], a_r.at[a, zz], along, z, c)

    def go_b(a, zz, dd):
        part = place(a, c, zz, dd, 1)
        return send(part, part, b_s.at[a, zz], b_r.at[a, zz], across, z, c)

    def pair(a, j, zz, cc, own=False):
        src = ins[a] if own else place(a, cc, zz, columns[j])
        return send(src, place(a, cc, zz, columns[j]), c_s.at[a, j, zz], c_r.at[a, j, zz], d, z, 1 - c)

    def spread(a, zz, own=False):
        if a < 2:
            go_x(a, zz, d, own).start()
            go_y(a, zz, d, own).start()
        pair(a, 0, zz, c, own).start()

    def line(a, distance):
        below, above = z - distance, z + distance

        @pl.when(below >= 0)
        def _():
            up(a, below).wait_recv()
            pl.when(z < chips - 1)(lambda: up(a, below).start())
            spread(a, below)

        @pl.when(above < chips)
        def _():
            down(a, above).wait_recv()
            pl.when(z > 0)(lambda: down(a, above).start())
            spread(a, above)

    def both(distance, act):
        for a in range(2):
            if distance == 0:
                act(a, z)
            else:
                pl.when(z - distance >= 0)(lambda: act(a, z - distance))
                pl.when(z + distance < chips)(lambda: act(a, z + distance))

    def plane(a, zz):
        go_x(a, zz, across).wait_recv()
        go_a(a, zz, across).start()
        pair(a, 1, zz, c).start()
        go_y(a, zz, along).wait_recv()
        go_b(a, zz, along).start()
        pair(a, 2, zz, c).start()

    def corner(a, zz):
        go_a(a, zz, diagonal).wait_recv()
        go_b(a, zz, diagonal).wait_recv()
        pair(a, 3, zz, c).start()

    greet(d, z, c, chips, across, along)
    for a in (2, 0, 1):
        pl.when(z < chips - 1)(lambda: up(a, z, True).start())
        pl.when(z > 0)(lambda: down(a, z, True).start())
        spread(a, z, True)
    locals_ = [pltpu.make_async_copy(ins[a], place(a, c, z, d), own_sem.at[a]) for a in range(3)]
    for copy in locals_:
        copy.start()
    for step in range(1, chips + 2):
        if step < chips:
            for a in (2, 0, 1):
                line(a, step)
        if step - 1 < chips:
            both(step - 1, plane)
        if 0 <= step - 2 < chips:
            both(step - 2, corner)
    for copy in locals_:
        copy.wait()
    for a in range(3):
        for zz in range(chips):
            for j in range(4 if a < 2 else 1):
                pair(a, j, zz, 1 - c).wait_recv()
                pair(a, j, zz, c).wait_send()
            if a < 2:
                go_x(a, zz, d).wait_send()
                go_y(a, zz, d).wait_send()
                go_a(a, zz, across).wait_send()
                go_b(a, zz, along).wait_send()
            pl.when((zz <= z) & (z < chips - 1))(lambda: up(a, zz).wait_send())
            pl.when((zz >= z) & (z > 0))(lambda: down(a, zz).wait_send())


def gather_all(tokens, grad_out, dense):
    count = lax.axis_size("expert")
    chips = count // CORES
    rows, width = tokens.shape
    whole = jax.ShapeDtypeStruct((count * rows, 4 * width), tokens.dtype)
    anywhere = pl.BlockSpec(memory_space=pl.ANY)
    dma = pltpu.SemaphoreType.DMA
    return pl.pallas_call(
        functools.partial(gather_kernel, chips),
        out_shape=(whole, whole, jax.ShapeDtypeStruct((count,) + dense.shape, dense.dtype)),
        in_specs=[anywhere] * 3,
        out_specs=(anywhere,) * 3,
        scratch_shapes=[dma((3,))]
        + [dma((3, chips))] * 3
        + [dma((2, chips))] * 8
        + [dma((3, 4, chips))] * 2,
        compiler_params=pltpu.CompilerParams(collective_id=0, has_side_effects=True),
        cost_estimate=pl.CostEstimate(flops=0, bytes_accessed=50_000_000, transcendentals=0),
    )(tokens, grad_out, dense)


def shards(tokens, expert_ids, route_weights, gate_weights, up_weights, down_weights, grad_out):
    count = lax.axis_size("expert")
    token_count = tokens.shape[0]
    me = lax.axis_index("expert")
    gate_weight = gate_weights[0]
    up_weight = up_weights[0]
    down_weight = down_weights[0]
    chosen = expert_ids[:, :, None] == jnp.arange(count, dtype=jnp.int32)
    dense = jnp.sum(jnp.where(chosen, route_weights[:, :, None], 0.0), axis=1)
    if lax.axis_size("dp") == 4 and count == 8:
        rows, grads, dense_all = gather_all(tokens, grad_out, dense.T)
        weight = lax.dynamic_index_in_dim(dense_all, me, axis=1, keepdims=False).reshape(-1, 1)
    else:
        dense_all = lax.all_gather(dense.T, "expert", axis=0)
        mine = lax.dynamic_index_in_dim(dense_all, me, axis=1, keepdims=False)
        weight = mine.reshape(count // CORES, CORES, token_count).transpose(1, 0, 2).reshape(-1, 1)
        rows = gather_rows(tokens)
        grads = gather_rows(grad_out)
    gate_pre = dot32(rows, gate_weight)
    up_pre = dot32(rows, up_weight)
    gate_sigmoid = jax.nn.sigmoid(gate_pre)
    hidden = gate_pre * gate_sigmoid * up_pre
    weighted = (weight * hidden).astype(jnp.bfloat16)
    mixed = scatter_rows(dot32(weighted, down_weight).astype(jnp.bfloat16))

    pulled = dot32(grads, down_weight, contract_last)
    route_part = jnp.sum(hidden * pulled, axis=1)
    hidden_grad = weight * pulled
    grad_gate_pre = (
        hidden_grad * up_pre * gate_sigmoid * (1.0 + gate_pre * (1.0 - gate_sigmoid))
    ).astype(jnp.bfloat16)
    grad_up_pre = (hidden_grad * gate_pre * gate_sigmoid).astype(jnp.bfloat16)
    row_part = (
        dot32(grad_gate_pre, gate_weight, contract_last)
        + dot32(grad_up_pre, up_weight, contract_last)
    ).astype(jnp.bfloat16)
    token_grad = scatter_rows(row_part)

    by_owner = route_part.reshape(CORES, count // CORES, token_count).transpose(1, 0, 2)
    own = lax.all_to_all(
        by_owner.reshape(count, token_count), "expert", split_axis=0, concat_axis=0, tiled=True
    )
    own = lax.psum(own, "dp")
    route_grad = jnp.sum(jnp.where(chosen, own.T[:, None, :], 0.0), axis=2)

    down_grad = dot32(weighted, grads, contract_first).astype(jnp.bfloat16)
    gate_grad = dot32(rows, grad_gate_pre, contract_first).astype(jnp.bfloat16)
    up_grad = dot32(rows, grad_up_pre, contract_first).astype(jnp.bfloat16)
    return (
        mixed,
        token_grad,
        route_grad,
        gate_grad[None],
        up_grad[None],
        down_grad[None],
    )


def solution(mesh):
    in_specs = (
        P("expert", "dp"),
        P("expert", None),
        P("expert", None),
        P("expert", None, "dp"),
        P("expert", None, "dp"),
        P("expert", "dp", None),
        P("expert", "dp"),
    )
    out_specs = (
        P("expert", "dp"),
        P("expert", "dp"),
        P("expert", None),
        P("expert", None, "dp"),
        P("expert", None, "dp"),
        P("expert", "dp", None),
    )
    return jax.shard_map(shards, mesh=mesh, in_specs=in_specs, out_specs=out_specs, check_vma=False)
```
